256 devices in a mesh: dp: 8 (over x_hi, y), ctx: 32 (over z, x_lo, core).
Axes of the slice: x: 4 (x_hi: 2, x_lo: 2; x = x_hi * 2 + x_lo), y: 4, z: 8, core: 2. Of those that a mesh axis runs over, the one named last changes fastest.
Arguments:
- queries: bfloat16 [65536, 512], P(('dp', 'ctx')), parts along dimension 0, may hold values from -60 to 60
- keys: bfloat16 [65536, 512], P(('dp', 'ctx')), parts along dimension 0, may hold values from -6 to 6
- values: bfloat16 [65536, 512], P(('dp', 'ctx')), parts along dimension 0, may hold values from -6 to 6
- grad_out: bfloat16 [65536, 512], P(('dp', 'ctx')), parts along dimension 0, may hold values from -6 to 6
- window: int32 [4], replicated, may hold values from 128 to 256, as said below
- offsets: int32 [1024, 4], P(('dp', 'ctx')), parts along dimension 0, may hold values from 5 to 67, as said below
Outputs:
- attended: bfloat16 [65536, 512], P(('dp', 'ctx')), parts along dimension 0
- grad_queries: bfloat16 [65536, 512], P(('dp', 'ctx')), parts along dimension 0
- grad_keys: bfloat16 [65536, 512], P(('dp', 'ctx')), parts along dimension 0
- grad_values: bfloat16 [65536, 512], P(('dp', 'ctx')), parts along dimension 0
The draws below stay inside these ranges and needn't reach their ends.
There are 8 independent parts, one for each index of `dp`. The reference program is written for one: setup_inputs(seed, part) draws one part's arguments, and reference() takes and returns one part's arrays. A program takes and returns all parts, laid end to end along the dimension named above; an argument that names none is the same for every part. Nothing has to cross between parts.
Inputs may be any that keep to these rules, and one draw needn't show every extreme that they name: `window`: every entry is between 128 and 256; some head has exactly 256 and some exactly 128. offsets[b, j] = 2 ** (j + 1) * 4 + (b % 4) - c with 0 <= c < 4, so the key block b - offsets[b, j] lies among the blocks of group b // 4 - 2 ** (j + 1).
All inputs are finite; a program needn't handle non-finite values.
Results may differ from the reference program's by a relative error of at most 0.017.
Values may be sent and summed in bfloat16 or wider, within the bound.
No kernel may reach another device: no remote copies, remote signals or barrier semaphores. Data moves between devices by JAX's collectives and lax.ppermute only.
A program may use at most 64 MiB of HBM per device.

```python
import jax
import jax.numpy as jnp
from jax import lax

HEADS = 4
HEAD_DIM = 128
FEAT = 512
TOK_DEV = 256
BLOCK = 64
LEVELS = 4
DOC_LEN = 8192
DOC_BLOCKS = 128
DEV_BLOCKS = 4
N_CTX = 32


def paired_rows(key):
    base = jax.random.fold_in(key, 7)
    key_a, key_b = jax.random.split(base, 2)
    row_total = DOC_LEN
    width = HEADS * HEAD_DIM
    key_rows = jnp.clip(jax.random.normal(key_a, (row_total, width), jnp.float32), -6.0, 6.0)
    query_rows = jnp.clip(2.0 * jax.random.normal(key_b, (row_total, width), jnp.float32), -12.0, 12.0)
    return (query_rows, key_rows)


def draw_queries(key, part):
    return paired_rows(key)[0].astype(jnp.bfloat16)


def draw_keys(key, part):
    return paired_rows(key)[1].astype(jnp.bfloat16)


def draw_window(key, part):
    key_a, key_b = jax.random.split(jax.random.fold_in(key, 3))
    lengths = jax.random.randint(key_a, (HEADS,), TOK_DEV // 2, TOK_DEV + 1)
    widest = jax.random.randint(key_b, (), 0, HEADS)
    heads_idx = jnp.arange(HEADS, dtype=jnp.int32)
    lengths = jnp.where(heads_idx == widest, TOK_DEV, lengths)
    lengths = jnp.where(heads_idx == (widest + 1) % HEADS, TOK_DEV // 2, lengths)
    return lengths.astype(jnp.int32)


def draw_offsets(key, part):
    jitter = jax.random.randint(jax.random.fold_in(key, 11), (DOC_BLOCKS, LEVELS), 0, DEV_BLOCKS)
    jitter = jitter.at[0, 0].set(DEV_BLOCKS - 1)
    jitter = jitter.at[DOC_BLOCKS - 1, LEVELS - 1].set(0)
    rows = jnp.arange(DOC_BLOCKS, dtype=jnp.int32)
    base = 2 ** (jnp.arange(LEVELS, dtype=jnp.int32) + 1) * DEV_BLOCKS
    return (base[None, :] + (rows % DEV_BLOCKS)[:, None] - jitter).astype(jnp.int32)


def block_levels(stream_key, shape, pieces, least, largest):
    gain, own = 1.0, jax.random.fold_in(stream_key, 6)
    for dim, parts in pieces:
        heights = jnp.exp(jax.random.uniform(jax.random.fold_in(own, dim), (parts,), jnp.float32, least / len(pieces), largest / len(pieces)))
        gain = gain * jnp.repeat(heights, shape[dim] // parts).reshape([-1 if axis == dim else 1 for axis in range(len(shape))])
    return gain


def scatter_about(stream_key, dims, scale, limit, cuts=(), kind=jnp.bfloat16):
    values = scale * jax.random.normal(stream_key, dims, jnp.float32)
    if cuts:
        values = values * block_levels(stream_key, dims, cuts, -0.22, 0.18)
    return jnp.clip(values, -limit, limit).astype(kind)


def setup_inputs(seed: int = 0, part: int = 0) -> dict:
    arg_keys = jax.random.split(jax.random.key(seed), 7)
    part_keys = jax.random.split(jax.random.fold_in(arg_keys[6], part), 7)
    return {
        "queries": draw_queries(jax.random.fold_in(jax.random.fold_in(arg_keys[6], part), 71), part),
        "keys": draw_keys(jax.random.fold_in(jax.random.fold_in(arg_keys[6], part), 71), part),
        "values": scatter_about(part_keys[2], (DOC_LEN, FEAT), 1.0, 6.0, ((0, 32),)),
        "grad_out": scatter_about(part_keys[3], (DOC_LEN, FEAT), 1.0, 6.0, ((0, 32),)),
        "window": draw_window(jax.random.fold_in(arg_keys[6], 71), part),
        "offsets": draw_offsets(jax.random.fold_in(jax.random.fold_in(arg_keys[6], part), 71), part),
    }


def local_pass(rank_index, query_rows, key_prev, key_own, value_prev, value_own, level_keys, level_values, grad_rows, window, offset_rows):
    row_count, feat_count = query_rows.shape
    head_count = window.shape[0]
    head_size = feat_count // head_count
    block_count = row_count // BLOCK
    score_scale = head_size ** -0.5
    query_pos = rank_index * row_count + jnp.arange(row_count, dtype=jnp.int32)
    key_pos = rank_index * row_count - row_count + jnp.arange(2 * row_count, dtype=jnp.int32)
    query_heads = query_rows.astype(jnp.float32).reshape(row_count, head_count, head_size)
    query_blocks = query_heads.reshape(block_count, BLOCK, head_count, head_size)
    grad_heads = grad_rows.astype(jnp.float32).reshape(row_count, head_count, head_size)
    grad_blocks = grad_heads.reshape(block_count, BLOCK, head_count, head_size)
    win_keys = jnp.concatenate([key_prev, key_own], 0).astype(jnp.float32).reshape(2 * row_count, head_count, head_size)
    win_values = jnp.concatenate([value_prev, value_own], 0).astype(jnp.float32).reshape(2 * row_count, head_count, head_size)
    block_ids = rank_index * block_count + jnp.arange(block_count, dtype=jnp.int32)
    picked_keys = []
    picked_values = []
    level_ok = []
    block_index = []
    for depth_index in range(LEVELS):
        source = rank_index - 2 ** (depth_index + 1)
        inside = jnp.clip(block_ids - offset_rows[:, depth_index] - source * block_count, 0, block_count - 1).astype(jnp.int32)
        block_index.append(inside)
        picked_keys.append(level_keys[depth_index].reshape(block_count, BLOCK, feat_count)[inside])
        picked_values.append(level_values[depth_index].reshape(block_count, BLOCK, feat_count)[inside])
        level_ok.append(jnp.broadcast_to(source >= 0, (BLOCK,)))
    log_width = LEVELS * BLOCK
    log_keys = jnp.stack(picked_keys, 1).astype(jnp.float32).reshape(block_count, log_width, head_count, head_size)
    log_values = jnp.stack(picked_values, 1).astype(jnp.float32).reshape(block_count, log_width, head_count, head_size)
    log_allowed = jnp.concatenate(level_ok, 0)
    win_scores = jnp.einsum('qhd,khd->hqk', query_heads, win_keys) * score_scale
    log_scores = jnp.einsum('pqhd,pkhd->hpqk', query_blocks, log_keys).reshape(head_count, row_count, log_width) * score_scale
    win_allowed = (key_pos[None, None, :] <= query_pos[None, :, None]) & (key_pos[None, None, :] > query_pos[None, :, None] - window[:, None, None]) & (key_pos[None, None, :] >= 0)
    allowed = jnp.concatenate([win_allowed, jnp.broadcast_to(log_allowed[None, None, :], (head_count, row_count, log_width))], -1)
    scores = jnp.where(allowed, jnp.concatenate([win_scores, log_scores], -1), jnp.float32(-1e30))
    top = jnp.max(scores, -1)
    weights = jnp.exp(scores - top[..., None])
    total = jnp.sum(weights, -1)
    weights_low = weights.astype(jnp.bfloat16).astype(jnp.float32)
    split_at = 2 * row_count
    out_win = jnp.einsum('hqk,khd->qhd', weights_low[..., :split_at], win_values)
    out_log = jnp.einsum('hpqk,pkhd->pqhd', weights_low[..., split_at:].reshape(head_count, block_count, BLOCK, log_width), log_values).reshape(row_count, head_count, head_size)
    attended = ((out_win + out_log) / total.T[:, :, None]).astype(jnp.bfloat16)
    lse = top + jnp.log(total)
    probs = jnp.exp(scores - lse[..., None])
    probs_low = probs.astype(jnp.bfloat16).astype(jnp.float32)
    delta = jnp.sum(grad_heads * attended.astype(jnp.float32), -1).T
    dprob_win = jnp.einsum('qhd,khd->hqk', grad_heads, win_values)
    dprob_log = jnp.einsum('pqhd,pkhd->hpqk', grad_blocks, log_values).reshape(head_count, row_count, log_width)
    dscore = probs * (jnp.concatenate([dprob_win, dprob_log], -1) - delta[..., None])
    dscore_low = dscore.astype(jnp.bfloat16).astype(jnp.float32)
    dscore_win = dscore_low[..., :split_at]
    dscore_log = dscore_low[..., split_at:].reshape(head_count, block_count, BLOCK, log_width)
    probs_win = probs_low[..., :split_at]
    probs_log = probs_low[..., split_at:].reshape(head_count, block_count, BLOCK, log_width)
    grad_q = (jnp.einsum('hqk,khd->qhd', dscore_win, win_keys) + jnp.einsum('hpqk,pkhd->pqhd', dscore_log, log_keys).reshape(row_count, head_count, head_size)) * score_scale
    grad_q = grad_q.astype(jnp.bfloat16).reshape(row_count, feat_count)
    dkey_win = (jnp.einsum('hqk,qhd->khd', dscore_win, query_heads) * score_scale).reshape(split_at, feat_count)
    dval_win = jnp.einsum('hqk,qhd->khd', probs_win, grad_heads).reshape(split_at, feat_count)
    dkey_log = (jnp.einsum('hpqk,pqhd->pkhd', dscore_log, query_blocks) * score_scale).reshape(block_count, LEVELS, BLOCK, feat_count)
    dval_log = jnp.einsum('hpqk,pqhd->pkhd', probs_log, grad_blocks).reshape(block_count, LEVELS, BLOCK, feat_count)
    level_dkey = []
    level_dval = []
    for depth_index in range(LEVELS):
        onehot = (block_index[depth_index][:, None] == jnp.arange(block_count, dtype=jnp.int32)[None, :]).astype(jnp.float32)
        level_dkey.append(jnp.einsum('pc,pkf->ckf', onehot, dkey_log[:, depth_index], precision=lax.Precision.HIGHEST).reshape(row_count, feat_count).astype(jnp.bfloat16))
        level_dval.append(jnp.einsum('pc,pkf->ckf', onehot, dval_log[:, depth_index], precision=lax.Precision.HIGHEST).reshape(row_count, feat_count).astype(jnp.bfloat16))
    return (attended.reshape(row_count, feat_count), grad_q, dkey_win[row_count:], dval_win[row_count:],
            dkey_win[:row_count].astype(jnp.bfloat16), dval_win[:row_count].astype(jnp.bfloat16),
            jnp.stack(level_dkey, 0), jnp.stack(level_dval, 0))


def shift_up(stacked, distance):
    if distance >= N_CTX:
        return jnp.zeros_like(stacked).astype(jnp.float32)
    tail = jnp.zeros((distance,) + stacked.shape[1:], jnp.float32)
    return jnp.concatenate([stacked[distance:].astype(jnp.float32), tail], 0)


def reference(queries, keys, values, grad_out, window, offsets):
    feat_count = queries.shape[1]
    row_count = TOK_DEV
    block_count = row_count // BLOCK
    margin = 2 ** LEVELS
    key_pad = jnp.concatenate([jnp.zeros((margin, row_count, feat_count), keys.dtype), keys.reshape(N_CTX, row_count, feat_count)], 0)
    value_pad = jnp.concatenate([jnp.zeros((margin, row_count, feat_count), values.dtype), values.reshape(N_CTX, row_count, feat_count)], 0)
    query_shards = queries.reshape(N_CTX, row_count, feat_count)
    grad_shards = grad_out.reshape(N_CTX, row_count, feat_count)

    def one_group(rank_index):
        pick = lambda table, back: lax.dynamic_index_in_dim(table, rank_index - back + margin, 0, keepdims=False)
        level_keys = [pick(key_pad, 2 ** (j + 1)) for j in range(LEVELS)]
        level_values = [pick(value_pad, 2 ** (j + 1)) for j in range(LEVELS)]
        offset_rows = lax.dynamic_slice_in_dim(offsets, (rank_index * block_count).astype(jnp.int32), block_count, 0)
        return local_pass(rank_index, query_shards[rank_index], pick(key_pad, 1), pick(key_pad, 0), pick(value_pad, 1), pick(value_pad, 0),
                          level_keys, level_values, grad_shards[rank_index], window, offset_rows)

    results = lax.map(one_group, jnp.arange(N_CTX, dtype=jnp.int32))
    attended, grad_q, own_dkey, own_dval, prev_dkey, prev_dval, lev_dkey, lev_dval = results
    grad_keys = own_dkey + shift_up(prev_dkey, 1)
    grad_values = own_dval + shift_up(prev_dval, 1)
    for j in range(LEVELS):
        grad_keys = grad_keys + shift_up(lev_dkey[:, j], 2 ** (j + 1))
        grad_values = grad_values + shift_up(lev_dval[:, j], 2 ** (j + 1))
    shape_out = (N_CTX * row_count, feat_count)
    return (attended.reshape(shape_out), grad_q.reshape(shape_out),
            grad_keys.astype(jnp.bfloat16).reshape(shape_out), grad_values.astype(jnp.bfloat16).reshape(shape_out))
```

```python
import functools

import jax
import jax.numpy as jnp
from jax import lax
from jax.experimental import pallas as pl
from jax.experimental.pallas import tpu as pltpu
from jax.sharding import PartitionSpec as P

HEADS = 4
HEAD_DIM = 128
FEAT = HEADS * HEAD_DIM
ROWS = 256
BLOCK = 64
BLOCKS = ROWS // BLOCK
LEVELS = 4
SCALE = HEAD_DIM**-0.5
WINDOW_COLS = ROWS + BLOCK
COLS = WINDOW_COLS + LEVELS * BLOCK
MASKED = -1e30
STAT_ROWS = 16
F32 = jnp.float32
BF16 = jnp.bfloat16


def rows_by_rows(a, b):
    return lax.dot_general(a, b, (((1,), (1,)), ((), ())), preferred_element_type=F32)


def rows_by_columns(a, b):
    return lax.dot_general(a, b, (((1,), (0,)), ((), ())), preferred_element_type=F32)


def query_side(win, off, qd, kv0, kv1, kv2, kv4, kv8, kv16, att, dq, stats, bias, tall):
    rank = lax.axis_index("ctx")
    far = (kv2, kv4, kv8, kv16)
    row = lax.broadcasted_iota(jnp.int32, (BLOCK, COLS), 0)
    col = lax.broadcasted_iota(jnp.int32, (BLOCK, COLS), 1)
    gap = col - row
    for h in range(HEADS):
        near = (gap <= ROWS) & (gap > ROWS - win[h])
        bias[h] = jnp.where(near | (col >= WINDOW_COLS), F32(0), F32(MASKED))
    lane = lax.broadcasted_iota(jnp.int32, (1, COLS), 1)
    stat_lane = lax.broadcasted_iota(jnp.int32, (BLOCK, 128), 1)
    for p in range(BLOCKS):
        need = jnp.where(lane + BLOCK * p < ROWS, 1, 0)
        for j in range(LEVELS):
            need = jnp.where(lane >= WINDOW_COLS + BLOCK * j, 2 ** (j + 1), need)
        exists = jnp.where(rank >= need, F32(0), F32(MASKED))
        picks = []
        for j in range(LEVELS):
            picked = jnp.clip(BLOCKS * 2 ** (j + 1) + p - off[p, j], 0, BLOCKS - 1)
            picks.append(pl.multiple_of(picked * BLOCK, BLOCK))
        mine = slice(BLOCK * p, BLOCK * (p + 1))
        kept = jnp.zeros((BLOCK, 128), F32)
        for h in range(HEADS):
            head = slice(HEAD_DIM * h, HEAD_DIM * (h + 1))

            def gathered(base):
                parts = [
                    kv1[base + BLOCK * p : base + ROWS, head],
                    kv0[base : base + BLOCK * (p + 1), head],
                ]
                for j in range(LEVELS):
                    parts.append(far[j][pl.ds(base + picks[j], BLOCK), head])
                return jnp.concatenate(parts, 0)

            k = gathered(0)
            v = gathered(ROWS)
            q = qd[mine, head]
            do = qd[ROWS + BLOCK * p : ROWS + BLOCK * (p + 1), head]
            scores = rows_by_rows(q, k) * SCALE + (bias[h] + exists)
            top = jnp.max(scores, 1, keepdims=True)
            weights = jnp.exp(scores - top)
            total = jnp.sum(weights, 1, keepdims=True)
            inverse = 1.0 / total
            out = (rows_by_columns(weights.astype(BF16), v) * inverse).astype(BF16)
            att[mine, head] = out
            delta = jnp.sum(do.astype(F32) * out.astype(F32), 1, keepdims=True)
            dscore = (weights * inverse) * (rows_by_rows(do, v) - delta)
            dq[mine, head] = (rows_by_columns(dscore.astype(BF16), k) * SCALE).astype(BF16)
            kept = jnp.where(stat_lane == h, top + jnp.log(total), kept)
            kept = jnp.where(stat_lane == HEADS + h, delta, kept)
        tall[mine, :] = kept
    stats[0 : 2 * HEADS, :] = tall[...].T[0 : 2 * HEADS]
    wide_row = lax.broadcasted_iota(jnp.int32, (STAT_ROWS - 2 * HEADS, ROWS), 0)
    wide_block = lax.broadcasted_iota(jnp.int32, (STAT_ROWS - 2 * HEADS, ROWS), 1) // BLOCK
    chosen = jnp.zeros((STAT_ROWS - 2 * HEADS, ROWS), F32)
    for p in range(BLOCKS):
        for j in range(LEVELS):
            picked = jnp.clip(BLOCKS * 2 ** (j + 1) + p - off[p, j], 0, BLOCKS - 1)
            chosen = jnp.where((wide_row == j) & (wide_block == p), picked.astype(F32), chosen)
    stats[2 * HEADS :, :] = chosen


def key_side(win, kv, qd0, qd1, qd2, qd4, qd8, qd16, st0, st1, st2, st4, st8, st16, dk, dv):
    far = ((qd2, st2), (qd4, st4), (qd8, st8), (qd16, st16))
    half = ROWS // 2
    wide = ROWS + half
    key_block = (lax.broadcasted_iota(jnp.int32, (ROWS, ROWS), 0) // BLOCK).astype(F32)
    row = lax.broadcasted_iota(jnp.int32, (half, wide), 0)
    col = lax.broadcasted_iota(jnp.int32, (half, wide), 1)
    gap = col - row
    for h in range(HEADS):
        head = slice(HEAD_DIM * h, HEAD_DIM * (h + 1))

        def pair(k, v, q, do, lse, delta, allowed):
            scores = rows_by_rows(k, q) * SCALE
            probs = jnp.exp(jnp.where(allowed, scores - lse, F32(MASKED)))
            dscore = probs * (rows_by_rows(v, do) - delta)
            return (
                rows_by_columns(dscore.astype(BF16), q),
                rows_by_columns(probs.astype(BF16), do),
            )

        near = []
        allowed = (gap >= 0) & (gap < win[h])
        for c in range(2):
            cut = half * c
            both = lambda a, b, base: jnp.concatenate(
                [a[base + cut : base + ROWS, head], b[base : base + cut + half, head]], 0
            )
            lanes = lambda r: jnp.concatenate([st0[r, cut:ROWS], st1[r, 0 : cut + half]], 0)[None, :]
            near.append(
                pair(
                    kv[cut : cut + half, head],
                    kv[ROWS + cut : ROWS + cut + half, head],
                    both(qd0, qd1, 0),
                    both(qd0, qd1, ROWS),
                    lanes(h),
                    lanes(HEADS + h),
                    allowed,
                )
            )
        dk_sum = jnp.concatenate([near[0][0], near[1][0]], 0)
        dv_sum = jnp.concatenate([near[0][1], near[1][1]], 0)
        for j in range(LEVELS):
            qd, st = far[j]
            dk_part, dv_part = pair(
                kv[0:ROWS, head],
                kv[ROWS : 2 * ROWS, head],
                qd[0:ROWS, head],
                qd[ROWS : 2 * ROWS, head],
                st[h : h + 1, :],
                st[HEADS + h : HEADS + h + 1, :],
                key_block == st[2 * HEADS + j : 2 * HEADS + j + 1, :],
            )
            dk_sum += dk_part
            dv_sum += dv_part
        dk[:, head] = (dk_sum * SCALE).astype(BF16)
        dv[:, head] = dv_sum.astype(BF16)


def moved(array, by):
    size = lax.axis_size("ctx")
    return lax.ppermute(array, "ctx", [(i, i + by) for i in range(size) if 0 <= i + by < size])


def on_device(queries, keys, values, grad_out, window, offsets):
    kv0 = jnp.concatenate([keys, values], 0)
    qd0 = jnp.concatenate([queries, grad_out], 0)
    kv4 = moved(kv0, 4)
    qd4 = moved(qd0, -4)
    kv2 = moved(kv0, 2)
    qd2 = moved(qd0, -2)
    kv1 = moved(kv0, 1)
    qd1 = moved(qd0, -1)
    kv8 = moved(kv4, 4)
    qd8 = moved(qd4, -4)
    kv16 = moved(kv8, 8)
    qd16 = moved(qd8, -8)
    smem = pl.BlockSpec(memory_space=pltpu.SMEM)
    vmem = pl.BlockSpec(memory_space=pltpu.VMEM)
    params = pltpu.CompilerParams(vmem_limit_bytes=32 * 2**20)
    half = jax.ShapeDtypeStruct((ROWS, FEAT), BF16)
    attended, grad_q, stats = pl.pallas_call(
        query_side,
        out_shape=(half, half, jax.ShapeDtypeStruct((STAT_ROWS, ROWS), F32)),
        in_specs=[smem, smem] + [vmem] * 7,
        out_specs=(vmem, vmem, vmem),
        scratch_shapes=[
            pltpu.VMEM((HEADS, BLOCK, COLS), F32),
            pltpu.VMEM((ROWS, 128), F32),
        ],
        compiler_params=params,
        cost_estimate=pl.CostEstimate(
            flops=8 * ROWS * COLS * FEAT, bytes_accessed=9 * ROWS * FEAT * 4, transcendentals=0
        ),
        name="query_side",
    )(window, offsets, qd0, kv0, kv1, kv2, kv4, kv8, kv16)
    received = [moved(stats, -by) for by in (1, 2, 4, 8, 16)]
    grad_k, grad_v = pl.pallas_call(
        key_side,
        out_shape=(half, half),
        in_specs=[smem] + [vmem] * 13,
        out_specs=(vmem, vmem),
        compiler_params=params,
        cost_estimate=pl.CostEstimate(
            flops=8 * ROWS * 6 * ROWS * FEAT, bytes_accessed=9 * ROWS * FEAT * 4, transcendentals=0
        ),
        name="key_side",
    )(window, kv0, qd0, qd1, qd2, qd4, qd8, qd16, stats, *received)
    return attended, grad_q, grad_k, grad_v


def solution(mesh):
    split = P(("dp", "ctx"), None)
    return jax.shard_map(
        on_device,
        mesh=mesh,
        in_specs=(split, split, split, split, P(), split),
        out_specs=(split,) * 4,
        check_vma=False,
    )
```

```python
import jax
import jax.numpy as jnp
from jax import lax
from jax.experimental import pallas as pl
from jax.experimental.pallas import tpu as pltpu
from jax.sharding import PartitionSpec as P

HEADS = 4
HEAD_DIM = 128
FEAT = HEADS * HEAD_DIM
ROWS = 256
BLOCK = 64
BLOCKS = ROWS // BLOCK
LEVELS = 4
SCALE = HEAD_DIM**-0.5
MASKED = -1e30
STAT_ROWS = 16
F32 = jnp.float32
BF16 = jnp.bfloat16


def rows_by_rows(a, b):
    return lax.dot_general(a, b, (((1,), (1,)), ((), ())), preferred_element_type=F32)


def rows_by_columns(a, b):
    return lax.dot_general(a, b, (((1,), (0,)), ((), ())), preferred_element_type=F32)


def picks_of(off, p):
    rows = []
    for j in range(LEVELS):
        picked = jnp.clip(BLOCKS * 2 ** (j + 1) + p - off[p, j], 0, BLOCKS - 1)
        rows.append(pl.multiple_of(picked * BLOCK, BLOCK))
    return rows


def block_keys(p, head, base, own, before, levels, picks):
    parts = []
    if before is not None:
        parts.append(before[base + BLOCK * p : base + ROWS, head])
    if own is not None:
        parts.append(own[base : base + BLOCK * (p + 1), head])
    for j, ref in levels:
        parts.append(ref[pl.ds(base + picks[j], BLOCK), head])
    return jnp.concatenate(parts, 0)


def block_bias(p, rank, length, own, before, levels):
    pieces = []
    row = lambda n: lax.broadcasted_iota(jnp.int32, (BLOCK, n), 0)
    col = lambda n: lax.broadcasted_iota(jnp.int32, (BLOCK, n), 1)
    if before:
        n = ROWS - BLOCK * p
        pieces.append((col(n) - row(n) > ROWS - length) & (rank > 0))
    if own:
        n = BLOCK * (p + 1)
        gap = BLOCK * p + row(n) - col(n)
        pieces.append((gap >= 0) & (gap < length))
    for j in levels:
        pieces.append((col(BLOCK) >= 0) & (rank >= 2 ** (j + 1)))
    return jnp.concatenate([jnp.where(x, F32(0), F32(MASKED)) for x in pieces], 1)


def across(column, width):
    return jnp.broadcast_to(column, (column.shape[0], width))


def widened(rows, width):
    return jnp.concatenate([rows] * (-(-width // 128)), 1)[:, :width]


def head_columns(h):
    return slice(HEAD_DIM * h, HEAD_DIM * (h + 1))


def with_ones(v):
    return jnp.concatenate([v, jnp.ones((v.shape[0], HEAD_DIM), BF16)], 1)


def early_attention(win, off, qd, kv0, kv4, kv8, acc, top_out, total_out):
    rank = lax.axis_index("ctx")
    levels = ((1, kv4), (2, kv8))
    heads = range(HEADS)
    for p in range(BLOCKS):
        picks = picks_of(off, p)
        mine = slice(BLOCK * p, BLOCK * (p + 1))
        k = [block_keys(p, head_columns(h), 0, kv0, None, levels, picks) for h in heads]
        v = [block_keys(p, head_columns(h), ROWS, kv0, None, levels, picks) for h in heads]
        width = k[0].shape[0]
        scores = [rows_by_rows(qd[mine, head_columns(h)], k[h]) for h in heads]
        scores = [scores[h] * SCALE + block_bias(p, rank, win[h], True, False, (1, 2)) for h in heads]
        top = [across(jnp.max(s, 1, keepdims=True), HEAD_DIM) for s in scores]
        weights = [jnp.exp(scores[h] - widened(top[h], width)).astype(BF16) for h in heads]
        sums = [rows_by_columns(weights[h], with_ones(v[h])) for h in heads]
        for h in heads:
            acc[mine, head_columns(h)] = sums[h][:, :HEAD_DIM]
            total_out[mine, head_columns(h)] = sums[h][:, HEAD_DIM:]
            top_out[mine, head_columns(h)] = top[h]


def late_attention(win, off, qd, kv1, kv2, kv16, acc, top0, total0, att, stats, tall):
    rank = lax.axis_index("ctx")
    levels = ((0, kv2), (3, kv16))
    heads = range(HEADS)
    lane = lax.broadcasted_iota(jnp.int32, (BLOCK, 128), 1)
    for p in range(BLOCKS):
        picks = picks_of(off, p)
        mine = slice(BLOCK * p, BLOCK * (p + 1))
        theirs = slice(ROWS + BLOCK * p, ROWS + BLOCK * (p + 1))
        k = [block_keys(p, head_columns(h), 0, None, kv1, levels, picks) for h in heads]
        v = [block_keys(p, head_columns(h), ROWS, None, kv1, levels, picks) for h in heads]
        width = k[0].shape[0]
        scores = [rows_by_rows(qd[mine, head_columns(h)], k[h]) for h in heads]
        scores = [scores[h] * SCALE + block_bias(p, rank, win[h], False, True, (0, 3)) for h in heads]
        before = [top0[mine, head_columns(h)] for h in heads]
        top = [jnp.maximum(before[h], across(jnp.max(scores[h], 1, keepdims=True), HEAD_DIM)) for h in heads]
        weights = [jnp.exp(scores[h] - widened(top[h], width)).astype(BF16) for h in heads]
        fade = [jnp.exp(before[h] - top[h]) for h in heads]
        sums = [rows_by_columns(weights[h], with_ones(v[h])) for h in heads]
        total = [total0[mine, head_columns(h)] * fade[h] + sums[h][:, HEAD_DIM:] for h in heads]
        out = [acc[mine, head_columns(h)] * fade[h] + sums[h][:, :HEAD_DIM] for h in heads]
        out = [(out[h] * (1.0 / total[h])).astype(BF16) for h in heads]
        lse = [top[h] + jnp.log(total[h]) for h in heads]
        delta = [
            across(jnp.sum(qd[theirs, head_columns(h)].astype(F32) * out[h].astype(F32), 1, keepdims=True), HEAD_DIM)
            for h in heads
        ]
        kept = jnp.zeros((BLOCK, 128), F32)
        for h in heads:
            att[mine, head_columns(h)] = out[h]
            kept = jnp.where(lane == h, lse[h], kept)
            kept = jnp.where(lane == HEADS + h, delta[h], kept)
        tall[mine, :] = kept
    stats[0 : 2 * HEADS, :] = tall[...].T[0 : 2 * HEADS]
    wide_row = lax.broadcasted_iota(jnp.int32, (STAT_ROWS - 2 * HEADS, ROWS), 0)
    wide_block = lax.broadcasted_iota(jnp.int32, (STAT_ROWS - 2 * HEADS, ROWS), 1) // BLOCK
    chosen = jnp.zeros((STAT_ROWS - 2 * HEADS, ROWS), F32)
    for p in range(BLOCKS):
        for j in range(LEVELS):
            picked = jnp.clip(BLOCKS * 2 ** (j + 1) + p - off[p, j], 0, BLOCKS - 1)
            chosen = jnp.where((wide_row == j) & (wide_block == p), picked.astype(F32), chosen)
    stats[2 * HEADS :, :] = chosen


def query_gradient(win, off, qd, kv0, kv1, kv2, kv4, kv8, kv16, tall, dq):
    rank = lax.axis_index("ctx")
    levels = ((0, kv2), (1, kv4), (2, kv8), (3, kv16))
    heads = range(HEADS)
    for p in range(BLOCKS):
        picks = picks_of(off, p)
        mine = slice(BLOCK * p, BLOCK * (p + 1))
        theirs = slice(ROWS + BLOCK * p, ROWS + BLOCK * (p + 1))
        k = [block_keys(p, head_columns(h), 0, kv0, kv1, levels, picks) for h in heads]
        v = [block_keys(p, head_columns(h), ROWS, kv0, kv1, levels, picks) for h in heads]
        scores = [rows_by_rows(qd[mine, head_columns(h)], k[h]) for h in heads]
        dprob = [rows_by_rows(qd[theirs, head_columns(h)], v[h]) for h in heads]
        scores = [scores[h] * SCALE + block_bias(p, rank, win[h], True, True, range(LEVELS)) for h in heads]
        probs = [jnp.exp(scores[h] - tall[mine, h : h + 1]) for h in heads]
        dscore = [(probs[h] * (dprob[h] - tall[mine, HEADS + h : HEADS + h + 1])).astype(BF16) for h in heads]
        for h in heads:
            dq[mine, head_columns(h)] = (rows_by_columns(dscore[h], k[h]) * SCALE).astype(BF16)


def key_side(win, kv, qd0, qd1, qd2, qd4, qd8, qd16, st0, st1, st2, st4, st8, st16, dk, dv):
    far = ((qd2, st2), (qd4, st4), (qd8, st8), (qd16, st16))
    half = ROWS // 2
    wide = ROWS + half
    key_block = (lax.broadcasted_iota(jnp.int32, (ROWS, ROWS), 0) // BLOCK).astype(F32)
    row = lax.broadcasted_iota(jnp.int32, (half, wide), 0)
    col = lax.broadcasted_iota(jnp.int32, (half, wide), 1)
    gap = col - row

    def tiles(h):
        head = head_columns(h)
        out = []
        allowed = (gap >= 0) & (gap < win[h])
        for c in range(2):
            cut = half * c
            both = lambda base: jnp.concatenate(
                [qd0[base + cut : base + ROWS, head], qd1[base : base + cut + half, head]], 0
            )
            lanes = lambda r: jnp.concatenate([st0[r : r + 1, cut:ROWS], st1[r : r + 1, 0 : cut + half]], 1)
            mine = slice(cut, cut + half)
            theirs = slice(ROWS + cut, ROWS + cut + half)
            out.append((kv[mine, head], kv[theirs, head], both(0), both(ROWS), lanes(h), lanes(HEADS + h), allowed))
        for j in range(LEVELS):
            qd, st = far[j]
            out.append(
                (
                    kv[0:ROWS, head],
                    kv[ROWS : 2 * ROWS, head],
                    qd[0:ROWS, head],
                    qd[ROWS : 2 * ROWS, head],
                    st[h : h + 1, :],
                    st[HEADS + h : HEADS + h + 1, :],
                    key_block == st[2 * HEADS + j : 2 * HEADS + j + 1, :],
                )
            )
        return out

    for h in range(HEADS):
        all_tiles = tiles(h)
        scores = [rows_by_rows(k, q) for k, _, q, _, _, _, _ in all_tiles]
        dprob = [rows_by_rows(v, do) for _, v, _, do, _, _, _ in all_tiles]
        probs = [
            jnp.exp(jnp.where(t[6], s * SCALE - t[4], F32(MASKED))) for s, t in zip(scores, all_tiles)
        ]
        dscore = [(p * (d - t[5])).astype(BF16) for p, d, t in zip(probs, dprob, all_tiles)]
        wide_q = jnp.concatenate([t[2] for t in all_tiles[2:]], 0)
        wide_do = jnp.concatenate([t[3] for t in all_tiles[2:]], 0)
        near_dv = jnp.concatenate([rows_by_columns(p.astype(BF16), t[3]) for p, t in zip(probs[:2], all_tiles)], 0)
        near_dk = jnp.concatenate([rows_by_columns(d, t[2]) for d, t in zip(dscore[:2], all_tiles)], 0)
        far_dv = rows_by_columns(jnp.concatenate([p.astype(BF16) for p in probs[2:]], 1), wide_do)
        far_dk = rows_by_columns(jnp.concatenate(dscore[2:], 1), wide_q)
        dk[:, head_columns(h)] = ((near_dk + far_dk) * SCALE).astype(BF16)
        dv[:, head_columns(h)] = (near_dv + far_dv).astype(BF16)


def moved(array, by):
    size = lax.axis_size("ctx")
    return lax.ppermute(array, "ctx", [(i, i + by) for i in range(size) if 0 <= i + by < size])


def swapped(array, bit):
    size = lax.axis_size("ctx")
    return lax.ppermute(array, "ctx", [(i, i ^ bit) for i in range(size)])


def kernel(body, out_shape, n_smem, n_vmem, flops, scratch=()):
    smem = pl.BlockSpec(memory_space=pltpu.SMEM)
    vmem = pl.BlockSpec(memory_space=pltpu.VMEM)
    return pl.pallas_call(
        body,
        out_shape=tuple(out_shape),
        in_specs=[smem] * n_smem + [vmem] * n_vmem,
        out_specs=(vmem,) * len(out_shape),
        scratch_shapes=list(scratch),
        compiler_params=pltpu.CompilerParams(vmem_limit_bytes=32 * 2**20),
        cost_estimate=pl.CostEstimate(flops=flops, bytes_accessed=n_vmem * ROWS * FEAT * 4, transcendentals=0),
        name=body.__name__,
    )


def on_device(queries, keys, values, grad_out, window, offsets):
    rank = lax.axis_index("ctx")
    kv0 = jnp.concatenate([keys, values], 0)
    qd0 = jnp.concatenate([queries, grad_out], 0)
    kv4 = moved(kv0, 4)
    qd4 = moved(qd0, -4)
    kv2 = swapped(jnp.where(rank % 4 < 2, kv0, kv4), 2)
    qd2 = swapped(jnp.where(rank % 4 < 2, qd4, qd0), 2)
    kv1 = swapped(jnp.where(rank % 2 == 0, kv0, kv2), 1)
    qd1 = swapped(jnp.where(rank % 2 == 0, qd2, qd0), 1)
    kv8 = moved(kv4, 4)
    qd8 = moved(qd4, -4)
    kv16 = moved(kv8, 8)
    qd16 = moved(qd8, -8)
    half = jax.ShapeDtypeStruct((ROWS, FEAT), BF16)
    whole = jax.ShapeDtypeStruct((ROWS, FEAT), F32)
    table = jax.ShapeDtypeStruct((ROWS, 128), F32)
    stat = jax.ShapeDtypeStruct((STAT_ROWS, ROWS), F32)
    unit = 2 * ROWS * FEAT
    early = kernel(early_attention, (whole,) * 3, 2, 4, unit * 2 * 320)(
        window, offsets, qd0, kv0, kv4, kv8
    )
    attended, stats, tall = kernel(late_attention, (half, stat, table), 2, 7, unit * 2 * 320)(
        window, offsets, qd0, kv1, kv2, kv16, *early
    )
    received = [moved(stats, -by) for by in (16, 8, 4, 2, 1)][::-1]
    (grad_q,) = kernel(query_gradient, (half,), 2, 8, unit * 3 * 576)(
        window, offsets, qd0, kv0, kv1, kv2, kv4, kv8, kv16, tall
    )
    grad_k, grad_v = kernel(key_side, (half, half), 1, 13, unit * 4 * 6 * ROWS)(
        window, kv0, qd0, qd1, qd2, qd4, qd8, qd16, stats, *received
    )
    return attended, grad_q, grad_k, grad_v


def solution(mesh):
    split = P(("dp", "ctx"), None)
    return jax.shard_map(
        on_device,
        mesh=mesh,
        in_specs=(split, split, split, split, P(), split),
        out_specs=(split,) * 4,
        check_vma=False,
    )
```

```python
import jax
import jax.numpy as jnp
from jax import lax
from jax.experimental import pallas as pl
from jax.experimental.pallas import tpu as pltpu
from jax.sharding import PartitionSpec as P

HEADS = 4
HEAD_DIM = 128
FEAT = HEADS * HEAD_DIM
ROWS = 256
BLOCK = 64
BLOCKS = ROWS // BLOCK
LEVELS = 4
SCALE = HEAD_DIM**-0.5
MASKED = -1e30
STAT_ROWS = 16
WINDOW = ROWS + BLOCK
FIRST = WINDOW + (LEVELS - 1) * BLOCK
HALF = ROWS // 2
WIDE = ROWS + HALF
F32 = jnp.float32
BF16 = jnp.bfloat16


def rows_by_rows(a, b):
    return lax.dot_general(a, b, (((1,), (1,)), ((), ())), preferred_element_type=F32)


def rows_by_columns(a, b):
    return lax.dot_general(a, b, (((1,), (0,)), ((), ())), preferred_element_type=F32)


def picks_of(off, p):
    rows = []
    for j in range(LEVELS):
        picked = jnp.clip(BLOCKS * 2 ** (j + 1) + p - off[p, j], 0, BLOCKS - 1)
        rows.append(pl.multiple_of(picked * BLOCK, BLOCK))
    return rows


def across(column, width):
    return jnp.broadcast_to(column, (column.shape[0], width))


def widened(rows, width):
    return jnp.concatenate([rows] * (-(-width // 128)), 1)[:, :width]


def head_columns(h):
    return slice(HEAD_DIM * h, HEAD_DIM * (h + 1))


def with_ones(v):
    return jnp.concatenate([v, jnp.ones((v.shape[0], HEAD_DIM), BF16)], 1)


def first_keys(p, head, base, own, before, levels, picks):
    parts = [before[base + BLOCK * p : base + ROWS, head], own[base : base + BLOCK * (p + 1), head]]
    for j, ref in enumerate(levels):
        parts.append(ref[pl.ds(base + picks[j], BLOCK), head])
    return jnp.concatenate(parts, 0)


def first_bias(p, rank, length):
    row = lax.broadcasted_iota(jnp.int32, (BLOCK, FIRST), 0)
    col = lax.broadcasted_iota(jnp.int32, (BLOCK, FIRST), 1)
    gap = col - row
    need = jnp.where(col + BLOCK * p < ROWS, 1, 0)
    for j in range(LEVELS - 1):
        need = jnp.where(col >= WINDOW + BLOCK * j, 2 ** (j + 1), need)
    near = (gap <= ROWS) & (gap > ROWS - length)
    return jnp.where((near | (col >= WINDOW)) & (rank >= need), F32(0), F32(MASKED))


def query_first(win, off, qd, kv0, kv1, kv2, kv4, kv8, scores_out, dprob_out, acc, top_out, total_out):
    rank = lax.axis_index("ctx")
    levels = (kv2, kv4, kv8)
    heads = range(HEADS)
    for p in range(BLOCKS):
        picks = picks_of(off, p)
        mine = slice(BLOCK * p, BLOCK * (p + 1))
        theirs = slice(ROWS + BLOCK * p, ROWS + BLOCK * (p + 1))
        k = [first_keys(p, head_columns(h), 0, kv0, kv1, levels, picks) for h in heads]
        v = [first_keys(p, head_columns(h), ROWS, kv0, kv1, levels, picks) for h in heads]
        scores = [rows_by_rows(qd[mine, head_columns(h)], k[h]) for h in heads]
        scores = [scores[h] * SCALE + first_bias(p, rank, win[h]) for h in heads]
        top = [across(jnp.max(s, 1, keepdims=True), HEAD_DIM) for s in scores]
        for h in heads:
            scores_out[h, mine, :] = scores[h]
            dprob_out[h, mine, :] = rows_by_rows(qd[theirs, head_columns(h)], v[h])
        weights = [jnp.exp(scores[h] - widened(top[h], FIRST)).astype(BF16) for h in heads]
        sums = [rows_by_columns(weights[h], with_ones(v[h])) for h in heads]
        for h in heads:
            acc[mine, head_columns(h)] = sums[h][:, :HEAD_DIM]
            total_out[mine, head_columns(h)] = sums[h][:, HEAD_DIM:]
            top_out[mine, head_columns(h)] = top[h]


def query_last(off, qd, kv16, acc, top0, total0, _, att, stats, lse_out, delta_out, tall):
    rank = lax.axis_index("ctx")
    heads = range(HEADS)
    lane = lax.broadcasted_iota(jnp.int32, (BLOCK, 128), 1)
    bias = jnp.where(rank >= 2**LEVELS, F32(0), F32(MASKED))
    tiles = [(p, h) for p in range(BLOCKS) for h in heads]
    picks = [picks_of(off, p)[LEVELS - 1] for p in range(BLOCKS)]
    rows = lambda p, base=0: slice(base + BLOCK * p, base + BLOCK * (p + 1))
    at = lambda ref, p, h: ref[rows(p), head_columns(h)]
    scores = [
        rows_by_rows(at(qd, p, h), kv16[pl.ds(picks[p], BLOCK), head_columns(h)]) * SCALE + bias for p, h in tiles
    ]
    before = [at(top0, p, h) for p, h in tiles]
    top = [jnp.maximum(b, across(jnp.max(s, 1, keepdims=True), HEAD_DIM)) for b, s in zip(before, scores)]
    weights = [jnp.exp(s - t[:, :BLOCK]).astype(BF16) for s, t in zip(scores, top)]
    sums = [
        rows_by_columns(w, with_ones(kv16[pl.ds(ROWS + picks[p], BLOCK), head_columns(h)]))
        for w, (p, h) in zip(weights, tiles)
    ]
    fade = [jnp.exp(b - t) for b, t in zip(before, top)]
    total = [at(total0, p, h) * f + x[:, HEAD_DIM:] for f, x, (p, h) in zip(fade, sums, tiles)]
    out = [at(acc, p, h) * f + x[:, :HEAD_DIM] for f, x, (p, h) in zip(fade, sums, tiles)]
    out = [(o * (1.0 / t)).astype(BF16) for o, t in zip(out, total)]
    lse = [t + jnp.log(x) for t, x in zip(top, total)]
    delta = [
        across(jnp.sum(qd[rows(p, ROWS), head_columns(h)].astype(F32) * o.astype(F32), 1, keepdims=True), HEAD_DIM)
        for o, (p, h) in zip(out, tiles)
    ]
    for p in range(BLOCKS):
        kept = jnp.zeros((BLOCK, 128), F32)
        for h in heads:
            i = p * HEADS + h
            att[rows(p), head_columns(h)] = out[i]
            lse_out[rows(p), head_columns(h)] = lse[i]
            delta_out[rows(p), head_columns(h)] = delta[i]
            kept = jnp.where(lane == h, lse[i], kept)
            kept = jnp.where(lane == HEADS + h, delta[i], kept)
        tall[rows(p), :] = kept
    stats[0 : 2 * HEADS, :] = tall[...].T[0 : 2 * HEADS]
    wide_row = lax.broadcasted_iota(jnp.int32, (STAT_ROWS - 2 * HEADS, ROWS), 0)
    wide_block = lax.broadcasted_iota(jnp.int32, (STAT_ROWS - 2 * HEADS, ROWS), 1) // BLOCK
    chosen = jnp.zeros((STAT_ROWS - 2 * HEADS, ROWS), F32)
    for p in range(BLOCKS):
        for j in range(LEVELS):
            picked = jnp.clip(BLOCKS * 2 ** (j + 1) + p - off[p, j], 0, BLOCKS - 1)
            chosen = jnp.where((wide_row == j) & (wide_block == p), picked.astype(F32), chosen)
    stats[2 * HEADS :, :] = chosen


def query_gradient(off, qd, kv0, kv1, kv2, kv4, kv8, kv16, scores, dprob, lse, delta, dq):
    rank = lax.axis_index("ctx")
    levels = (kv2, kv4, kv8)
    heads = range(HEADS)
    bias = jnp.where(rank >= 2**LEVELS, F32(0), F32(MASKED))
    for p in range(BLOCKS):
        picks = picks_of(off, p)
        mine = slice(BLOCK * p, BLOCK * (p + 1))
        theirs = slice(ROWS + BLOCK * p, ROWS + BLOCK * (p + 1))
        k = [first_keys(p, head_columns(h), 0, kv0, kv1, levels, picks) for h in heads]
        last_k = [kv16[pl.ds(picks[-1], BLOCK), head_columns(h)] for h in heads]
        last_v = [kv16[pl.ds(ROWS + picks[-1], BLOCK), head_columns(h)] for h in heads]
        last = [rows_by_rows(qd[mine, head_columns(h)], last_k[h]) * SCALE + bias for h in heads]
        last_dprob = [rows_by_rows(qd[theirs, head_columns(h)], last_v[h]) for h in heads]
        my_lse = [lse[mine, head_columns(h)] for h in heads]
        my_delta = [delta[mine, head_columns(h)] for h in heads]
        first = [
            jnp.exp(scores[h, mine, :] - widened(my_lse[h], FIRST)) * (dprob[h, mine, :] - widened(my_delta[h], FIRST))
            for h in heads
        ]
        last = [jnp.exp(last[h] - my_lse[h][:, :BLOCK]) * (last_dprob[h] - my_delta[h][:, :BLOCK]) for h in heads]
        for h in heads:
            total = rows_by_columns(first[h].astype(BF16), k[h]) + rows_by_columns(last[h].astype(BF16), last_k[h])
            dq[mine, head_columns(h)] = (total * SCALE).astype(BF16)


def joined(a, b, base, cut, head):
    return jnp.concatenate([a[base + cut : base + ROWS, head], b[base : base + cut + HALF, head]], 0)


def key_first(kv, qd2, qd4, qd8, scores, dprob):
    for h in range(HEADS):
        head = head_columns(h)
        for j, qd in enumerate((qd2, qd4, qd8)):
            columns = slice(ROWS * j, ROWS * (j + 1))
            scores[h, :, columns] = rows_by_rows(kv[0:ROWS, head], qd[0:ROWS, head]) * SCALE
            dprob[h, :, columns] = rows_by_rows(kv[ROWS : 2 * ROWS, head], qd[ROWS : 2 * ROWS, head])


def key_last(
    win, kv, qd0, qd1, qd2, qd4, qd8, qd16, far_scores, far_dprob, st16, st8, st4, st2, st1, st0, dk, dv
):
    key_block = (lax.broadcasted_iota(jnp.int32, (ROWS, ROWS), 0) // BLOCK).astype(F32)
    far = ((qd2, st2), (qd4, st4), (qd8, st8), (qd16, st16))
    row = lax.broadcasted_iota(jnp.int32, (HALF, WIDE), 0)
    col = lax.broadcasted_iota(jnp.int32, (HALF, WIDE), 1)
    gap = col - row
    chosen = [key_block == st[2 * HEADS + j : 2 * HEADS + j + 1, :] for j, (_, st) in enumerate(far)]
    for h in range(HEADS):
        head = head_columns(h)
        lanes = lambda r, cut: jnp.concatenate([st0[r : r + 1, cut:ROWS], st1[r : r + 1, 0 : cut + HALF]], 1)
        bias = jnp.where((gap >= 0) & (gap < win[h]), F32(0), F32(MASKED))
        scores = [
            rows_by_rows(kv[HALF * c : HALF * (c + 1), head], joined(qd0, qd1, 0, HALF * c, head)) * SCALE + bias
            for c in range(2)
        ]
        dprob = [
            rows_by_rows(kv[ROWS + HALF * c : ROWS + HALF * (c + 1), head], joined(qd0, qd1, ROWS, HALF * c, head))
            for c in range(2)
        ]
        scores += [far_scores[h, :, ROWS * j : ROWS * (j + 1)] for j in range(LEVELS - 1)]
        dprob += [far_dprob[h, :, ROWS * j : ROWS * (j + 1)] for j in range(LEVELS - 1)]
        scores.append(rows_by_rows(kv[0:ROWS, head], qd16[0:ROWS, head]) * SCALE)
        dprob.append(rows_by_rows(kv[ROWS : 2 * ROWS, head], qd16[ROWS : 2 * ROWS, head]))
        lse = [lanes(h, HALF * c) for c in range(2)] + [st[h : h + 1, :] for _, st in far]
        delta = [lanes(HEADS + h, HALF * c) for c in range(2)]
        delta += [st[HEADS + h : HEADS + h + 1, :] for _, st in far]
        probs = [jnp.exp(scores[i] - lse[i]) for i in range(2)]
        probs += [jnp.exp(jnp.where(chosen[j], scores[2 + j] - lse[2 + j], F32(MASKED))) for j in range(LEVELS)]
        dscore = [(probs[i] * (dprob[i] - delta[i])).astype(BF16) for i in range(2 + LEVELS)]
        probs = [x.astype(BF16) for x in probs]
        for rows, base, out, scale in ((dscore, 0, dk, SCALE), (probs, ROWS, dv, 1.0)):
            near = [rows_by_columns(rows[c], joined(qd0, qd1, base, HALF * c, head)) for c in range(2)]
            stack = jnp.concatenate([qd[base : base + ROWS, head] for qd, _ in far], 0)
            total = jnp.concatenate(near, 0) + rows_by_columns(jnp.concatenate(rows[2:], 1), stack)
            out[:, head] = (total * scale).astype(BF16)


def moved(array, by):
    size = lax.axis_size("ctx")
    return lax.ppermute(array, "ctx", [(i, i + by) for i in range(size) if 0 <= i + by < size])


def swapped(array, bit):
    size = lax.axis_size("ctx")
    return lax.ppermute(array, "ctx", [(i, i ^ bit) for i in range(size)])


def kernel(body, out_shape, n_smem, n_vmem, flops, scratch=(), n_any=0):
    smem = pl.BlockSpec(memory_space=pltpu.SMEM)
    vmem = pl.BlockSpec(memory_space=pltpu.VMEM)
    return pl.pallas_call(
        body,
        out_shape=tuple(out_shape),
        in_specs=[smem] * n_smem + [vmem] * n_vmem + [pl.BlockSpec(memory_space=pl.ANY)] * n_any,
        out_specs=(vmem,) * len(out_shape),
        scratch_shapes=list(scratch),
        compiler_params=pltpu.CompilerParams(vmem_limit_bytes=32 * 2**20),
        cost_estimate=pl.CostEstimate(flops=flops, bytes_accessed=n_vmem * ROWS * FEAT * 4, transcendentals=0),
        name=body.__name__,
    )


def on_device(queries, keys, values, grad_out, window, offsets):
    rank = lax.axis_index("ctx")
    kv0 = jnp.concatenate([keys, values], 0)
    qd0 = jnp.concatenate([queries, grad_out], 0)
    kv4 = moved(kv0, 4)
    qd4 = moved(qd0, -4)
    kv2 = swapped(jnp.where(rank % 4 < 2, kv0, kv4), 2)
    qd2 = swapped(jnp.where(rank % 4 < 2, qd4, qd0), 2)
    kv1 = swapped(jnp.where(rank % 2 == 0, kv0, kv2), 1)
    qd1 = swapped(jnp.where(rank % 2 == 0, qd2, qd0), 1)
    kv8 = moved(kv4, 4)
    qd8 = moved(qd4, -4)
    kv16 = moved(kv8, 8)
    qd16 = moved(qd8, -8)
    half = jax.ShapeDtypeStruct((ROWS, FEAT), BF16)
    f32 = lambda *shape: jax.ShapeDtypeStruct(shape, F32)
    unit = 2 * ROWS * FEAT
    scores, dprob, *sums = kernel(
        query_first, (f32(HEADS, ROWS, FIRST), f32(HEADS, ROWS, FIRST)) + (f32(ROWS, FEAT),) * 3, 2, 6, unit * 3 * FIRST
    )(window, offsets, qd0, kv0, kv1, kv2, kv4, kv8)
    pre = kernel(key_first, (f32(HEADS, ROWS, 3 * ROWS),) * 2, 0, 4, unit * 2 * 3 * ROWS)(kv0, qd2, qd4, qd8)
    attended, stats, lse, delta = kernel(
        query_last,
        (half, f32(STAT_ROWS, ROWS), f32(ROWS, FEAT), f32(ROWS, FEAT)),
        1,
        5,
        unit * 2 * BLOCK,
        (pltpu.VMEM((ROWS, 128), F32),),
        n_any=1,
    )(offsets, qd0, kv16, *sums, pre[1])
    received = [moved(stats, -by) for by in (1, 2, 4, 8, 16)]
    (grad_q,) = kernel(query_gradient, (half,), 1, 11, unit * FIRST)(
        offsets, qd0, kv0, kv1, kv2, kv4, kv8, kv16, scores, dprob, lse, delta
    )
    grad_k, grad_v = kernel(key_last, (half, half), 1, 15, unit * 2 * 6 * ROWS)(
        window, kv0, qd0, qd1, qd2, qd4, qd8, qd16, *pre, *received[::-1], stats
    )
    return attended, grad_q, grad_k, grad_v


def solution(mesh):
    split = P(("dp", "ctx"), None)
    return jax.shard_map(
        on_device,
        mesh=mesh,
        in_specs=(split, split, split, split, P(), split),
        out_specs=(split,) * 4,
        check_vma=False,
    )
```

```python
import jax
import jax.numpy as jnp
from jax import lax
from jax.experimental import pallas as pl
from jax.experimental.pallas import tpu as pltpu
from jax.sharding import PartitionSpec as P

HEADS = 4
HEAD_DIM = 128
FEAT = HEADS * HEAD_DIM
ROWS = 256
BLOCK = 64
BLOCKS = ROWS // BLOCK
LEVELS = 4
SCALE = HEAD_DIM**-0.5
MASKED = -1e30
STAT_ROWS = 16
WINDOW = ROWS + BLOCK
FIRST = WINDOW + (LEVELS - 1) * BLOCK
HALF = ROWS // 2
WIDE = ROWS + HALF
F32 = jnp.float32
BF16 = jnp.bfloat16


def rows_by_rows(a, b):
    return lax.dot_general(a, b, (((1,), (1,)), ((), ())), preferred_element_type=F32)


def rows_by_columns(a, b):
    return lax.dot_general(a, b, (((1,), (0,)), ((), ())), preferred_element_type=F32)


class Rows:
    def __init__(self, top, bottom):
        self.top, self.bottom = top, bottom

    def __getitem__(self, index):
        rows, columns = index
        if rows.start >= ROWS:
            return self.bottom[rows.start - ROWS : rows.stop - ROWS, columns]
        return self.top[rows, columns]


def picks_of(off, p):
    rows = []
    for j in range(LEVELS):
        picked = jnp.clip(BLOCKS * 2 ** (j + 1) + p - off[p, j], 0, BLOCKS - 1)
        rows.append(pl.multiple_of(picked * BLOCK, BLOCK))
    return rows


def across(column, width):
    return jnp.broadcast_to(column, (column.shape[0], width))


def widened(rows, width):
    return jnp.concatenate([rows] * (-(-width // 128)), 1)[:, :width]


def head_columns(h):
    return slice(HEAD_DIM * h, HEAD_DIM * (h + 1))


def with_ones(v):
    return jnp.concatenate([v, jnp.ones((v.shape[0], HEAD_DIM), BF16)], 1)


def first_keys(p, head, base, own, before, levels, picks):
    parts = [before[base + BLOCK * p : base + ROWS, head], own[base : base + BLOCK * (p + 1), head]]
    for j, ref in enumerate(levels):
        parts.append(ref[pl.ds(base + picks[j], BLOCK), head])
    return jnp.concatenate(parts, 0)


def first_bias(p, rank, length):
    row = lax.broadcasted_iota(jnp.int32, (BLOCK, FIRST), 0)
    col = lax.broadcasted_iota(jnp.int32, (BLOCK, FIRST), 1)
    gap = col - row
    need = jnp.where(col + BLOCK * p < ROWS, 1, 0)
    for j in range(LEVELS - 1):
        need = jnp.where(col >= WINDOW + BLOCK * j, 2 ** (j + 1), need)
    near = (gap <= ROWS) & (gap > ROWS - length)
    return jnp.where((near | (col >= WINDOW)) & (rank >= need), F32(0), F32(MASKED))


def query_first(win, off, q, do, k0, v0, kv1, kv2, kv4, kv8, scores_out, dprob_out, acc, top_out, total_out):
    rank = lax.axis_index("ctx")
    levels = (kv2, kv4, kv8)
    heads = range(HEADS)
    qd, kv0 = Rows(q, do), Rows(k0, v0)
    for p in range(BLOCKS):
        picks = picks_of(off, p)
        mine = slice(BLOCK * p, BLOCK * (p + 1))
        theirs = slice(ROWS + BLOCK * p, ROWS + BLOCK * (p + 1))
        k = [first_keys(p, head_columns(h), 0, kv0, kv1, levels, picks) for h in heads]
        v = [first_keys(p, head_columns(h), ROWS, kv0, kv1, levels, picks) for h in heads]
        scores = [rows_by_rows(qd[mine, head_columns(h)], k[h]) for h in heads]
        scores = [scores[h] * SCALE + first_bias(p, rank, win[h]) for h in heads]
        top = [across(jnp.max(s, 1, keepdims=True), HEAD_DIM) for s in scores]
        for h in heads:
            scores_out[h, mine, :] = scores[h]
            dprob_out[h, mine, :] = rows_by_rows(qd[theirs, head_columns(h)], v[h])
        weights = [jnp.exp(scores[h] - widened(top[h], FIRST)).astype(BF16) for h in heads]
        sums = [rows_by_columns(weights[h], with_ones(v[h])) for h in heads]
        for h in heads:
            acc[mine, head_columns(h)] = sums[h][:, :HEAD_DIM]
            total_out[mine, head_columns(h)] = sums[h][:, HEAD_DIM:]
            top_out[mine, head_columns(h)] = top[h]


def query_last(off, q, do, kv16, acc, top0, total0, _, att, stats, lse_out, delta_out, tall):
    rank = lax.axis_index("ctx")
    heads = range(HEADS)
    qd = Rows(q, do)
    lane = lax.broadcasted_iota(jnp.int32, (BLOCK, 128), 1)
    bias = jnp.where(rank >= 2**LEVELS, F32(0), F32(MASKED))
    tiles = [(p, h) for p in range(BLOCKS) for h in heads]
    picks = [picks_of(off, p)[LEVELS - 1] for p in range(BLOCKS)]
    rows = lambda p, base=0: slice(base + BLOCK * p, base + BLOCK * (p + 1))
    at = lambda ref, p, h: ref[rows(p), head_columns(h)]
    scores = [
        rows_by_rows(at(qd, p, h), kv16[pl.ds(picks[p], BLOCK), head_columns(h)]) * SCALE + bias for p, h in tiles
    ]
    before = [at(top0, p, h) for p, h in tiles]
    top = [jnp.maximum(b, across(jnp.max(s, 1, keepdims=True), HEAD_DIM)) for b, s in zip(before, scores)]
    weights = [jnp.exp(s - t[:, :BLOCK]).astype(BF16) for s, t in zip(scores, top)]
    sums = [
        rows_by_columns(w, with_ones(kv16[pl.ds(ROWS + picks[p], BLOCK), head_columns(h)]))
        for w, (p, h) in zip(weights, tiles)
    ]
    fade = [jnp.exp(b - t) for b, t in zip(before, top)]
    total = [at(total0, p, h) * f + x[:, HEAD_DIM:] for f, x, (p, h) in zip(fade, sums, tiles)]
    out = [at(acc, p, h) * f + x[:, :HEAD_DIM] for f, x, (p, h) in zip(fade, sums, tiles)]
    out = [(o * (1.0 / t)).astype(BF16) for o, t in zip(out, total)]
    lse = [t + jnp.log(x) for t, x in zip(top, total)]
    delta = [
        across(jnp.sum(qd[rows(p, ROWS), head_columns(h)].astype(F32) * o.astype(F32), 1, keepdims=True), HEAD_DIM)
        for o, (p, h) in zip(out, tiles)
    ]
    for p in range(BLOCKS):
        kept = jnp.zeros((BLOCK, 128), F32)
        for h in heads:
            i = p * HEADS + h
            att[rows(p), head_columns(h)] = out[i]
            lse_out[rows(p), head_columns(h)] = lse[i]
            delta_out[rows(p), head_columns(h)] = delta[i]
            kept = jnp.where(lane == h, lse[i], kept)
            kept = jnp.where(lane == HEADS + h, delta[i], kept)
        tall[rows(p), :] = kept
    stats[0 : 2 * HEADS, :] = tall[...].T[0 : 2 * HEADS]
    wide_row = lax.broadcasted_iota(jnp.int32, (STAT_ROWS - 2 * HEADS, ROWS), 0)
    wide_block = lax.broadcasted_iota(jnp.int32, (STAT_ROWS - 2 * HEADS, ROWS), 1) // BLOCK
    chosen = jnp.zeros((STAT_ROWS - 2 * HEADS, ROWS), F32)
    for p in range(BLOCKS):
        for j in range(LEVELS):
            picked = jnp.clip(BLOCKS * 2 ** (j + 1) + p - off[p, j], 0, BLOCKS - 1)
            chosen = jnp.where((wide_row == j) & (wide_block == p), picked.astype(F32), chosen)
    stats[2 * HEADS :, :] = chosen


def query_gradient(off, q, do, k0, v0, kv1, kv2, kv4, kv8, kv16, scores, dprob, lse, delta, dq):
    rank = lax.axis_index("ctx")
    levels = (kv2, kv4, kv8)
    qd, kv0 = Rows(q, do), Rows(k0, v0)
    heads = range(HEADS)
    bias = jnp.where(rank >= 2**LEVELS, F32(0), F32(MASKED))
    for p in range(BLOCKS):
        picks = picks_of(off, p)
        mine = slice(BLOCK * p, BLOCK * (p + 1))
        theirs = slice(ROWS + BLOCK * p, ROWS + BLOCK * (p + 1))
        k = [first_keys(p, head_columns(h), 0, kv0, kv1, levels, picks) for h in heads]
        last_k = [kv16[pl.ds(picks[-1], BLOCK), head_columns(h)] for h in heads]
        last_v = [kv16[pl.ds(ROWS + picks[-1], BLOCK), head_columns(h)] for h in heads]
        last = [rows_by_rows(qd[mine, head_columns(h)], last_k[h]) * SCALE + bias for h in heads]
        last_dprob = [rows_by_rows(qd[theirs, head_columns(h)], last_v[h]) for h in heads]
        my_lse = [lse[mine, head_columns(h)] for h in heads]
        my_delta = [delta[mine, head_columns(h)] for h in heads]
        first = [
            jnp.exp(scores[h, mine, :] - widened(my_lse[h], FIRST)) * (dprob[h, mine, :] - widened(my_delta[h], FIRST))
            for h in heads
        ]
        last = [jnp.exp(last[h] - my_lse[h][:, :BLOCK]) * (last_dprob[h] - my_delta[h][:, :BLOCK]) for h in heads]
        for h in heads:
            total = rows_by_columns(first[h].astype(BF16), k[h]) + rows_by_columns(last[h].astype(BF16), last_k[h])
            dq[mine, head_columns(h)] = (total * SCALE).astype(BF16)


def joined(a, b, base, cut, head):
    return jnp.concatenate([a[base + cut : base + ROWS, head], b[base : base + cut + HALF, head]], 0)


def key_first(k0, v0, qd2, qd4, qd8, scores, dprob):
    kv = Rows(k0, v0)
    for h in range(HEADS):
        head = head_columns(h)
        for j, qd in enumerate((qd2, qd4, qd8)):
            columns = slice(ROWS * j, ROWS * (j + 1))
            scores[h, :, columns] = rows_by_rows(kv[0:ROWS, head], qd[0:ROWS, head]) * SCALE
            dprob[h, :, columns] = rows_by_rows(kv[ROWS : 2 * ROWS, head], qd[ROWS : 2 * ROWS, head])


def key_last(
    win, k0, v0, q0, do0, qd1, qd2, qd4, qd8, qd16, far_scores, far_dprob, st16, st8, st4, st2, st1, st0, dk, dv
):
    kv, qd0 = Rows(k0, v0), Rows(q0, do0)
    key_block = (lax.broadcasted_iota(jnp.int32, (ROWS, ROWS), 0) // BLOCK).astype(F32)
    far = ((qd2, st2), (qd4, st4), (qd8, st8), (qd16, st16))
    row = lax.broadcasted_iota(jnp.int32, (HALF, WIDE), 0)
    col = lax.broadcasted_iota(jnp.int32, (HALF, WIDE), 1)
    gap = col - row
    chosen = [key_block == st[2 * HEADS + j : 2 * HEADS + j + 1, :] for j, (_, st) in enumerate(far)]
    for h in range(HEADS):
        head = head_columns(h)
        lanes = lambda r, cut: jnp.concatenate([st0[r : r + 1, cut:ROWS], st1[r : r + 1, 0 : cut + HALF]], 1)
        bias = jnp.where((gap >= 0) & (gap < win[h]), F32(0), F32(MASKED))
        scores = [
            rows_by_rows(kv[HALF * c : HALF * (c + 1), head], joined(qd0, qd1, 0, HALF * c, head)) * SCALE + bias
            for c in range(2)
        ]
        dprob = [
            rows_by_rows(kv[ROWS + HALF * c : ROWS + HALF * (c + 1), head], joined(qd0, qd1, ROWS, HALF * c, head))
            for c in range(2)
        ]
        scores += [far_scores[h, :, ROWS * j : ROWS * (j + 1)] for j in range(LEVELS - 1)]
        dprob += [far_dprob[h, :, ROWS * j : ROWS * (j + 1)] for j in range(LEVELS - 1)]
        scores.append(rows_by_rows(kv[0:ROWS, head], qd16[0:ROWS, head]) * SCALE)
        dprob.append(rows_by_rows(kv[ROWS : 2 * ROWS, head], qd16[ROWS : 2 * ROWS, head]))
        lse = [lanes(h, HALF * c) for c in range(2)] + [st[h : h + 1, :] for _, st in far]
        delta = [lanes(HEADS + h, HALF * c) for c in range(2)]
        delta += [st[HEADS + h : HEADS + h + 1, :] for _, st in far]
        probs = [jnp.exp(scores[i] - lse[i]) for i in range(2)]
        probs += [jnp.exp(jnp.where(chosen[j], scores[2 + j] - lse[2 + j], F32(MASKED))) for j in range(LEVELS)]
        dscore = [(probs[i] * (dprob[i] - delta[i])).astype(BF16) for i in range(2 + LEVELS)]
        probs = [x.astype(BF16) for x in probs]
        for rows, base, out, scale in ((dscore, 0, dk, SCALE), (probs, ROWS, dv, 1.0)):
            near = [rows_by_columns(rows[c], joined(qd0, qd1, base, HALF * c, head)) for c in range(2)]
            stack = jnp.concatenate([qd[base : base + ROWS, head] for qd, _ in far], 0)
            total = jnp.concatenate(near, 0) + rows_by_columns(jnp.concatenate(rows[2:], 1), stack)
            out[:, head] = (total * scale).astype(BF16)


def moved(array, by):
    size = lax.axis_size("ctx")
    return lax.ppermute(array, "ctx", [(i, i + by) for i in range(size) if 0 <= i + by < size])


def swapped(array, bit):
    size = lax.axis_size("ctx")
    return lax.ppermute(array, "ctx", [(i, i ^ bit) for i in range(size)])


def passed(array):
    anywhere = pl.BlockSpec(memory_space=pl.ANY)
    return pl.pallas_call(
        lambda a, b: None,
        out_shape=jax.ShapeDtypeStruct(array.shape, array.dtype),
        in_specs=[anywhere],
        out_specs=anywhere,
        input_output_aliases={0: 0},
        compiler_params=pltpu.CompilerParams(vmem_limit_bytes=2**20),
        cost_estimate=pl.CostEstimate(flops=10**10, bytes_accessed=4 * 10**7, transcendentals=0),
        name="passed",
    )(array)


def kernel(body, out_shape, n_smem, n_vmem, flops, scratch=(), n_any=0):
    smem = pl.BlockSpec(memory_space=pltpu.SMEM)
    vmem = pl.BlockSpec(memory_space=pltpu.VMEM)
    return pl.pallas_call(
        body,
        out_shape=tuple(out_shape),
        in_specs=[smem] * n_smem + [vmem] * n_vmem + [pl.BlockSpec(memory_space=pl.ANY)] * n_any,
        out_specs=(vmem,) * len(out_shape),
        scratch_shapes=list(scratch),
        compiler_params=pltpu.CompilerParams(vmem_limit_bytes=32 * 2**20),
        cost_estimate=pl.CostEstimate(flops=flops, bytes_accessed=n_vmem * ROWS * FEAT * 4, transcendentals=0),
        name=body.__name__,
    )


def on_device(queries, keys, values, grad_out, window, offsets):
    rank = lax.axis_index("ctx")
    kv0 = jnp.concatenate([keys, values], 0)
    qd0 = jnp.concatenate([queries, grad_out], 0)
    kv4 = moved(kv0, 4)
    qd4 = moved(qd0, -4)
    kv2 = swapped(jnp.where(rank % 4 < 2, kv0, kv4), 2)
    qd2 = swapped(jnp.where(rank % 4 < 2, qd4, qd0), 2)
    kv1 = swapped(jnp.where(rank % 2 == 0, kv0, kv2), 1)
    qd1 = swapped(jnp.where(rank % 2 == 0, qd2, qd0), 1)
    kv8 = passed(moved(kv4, 4))
    qd8 = passed(moved(qd4, -4))
    kv16 = moved(kv8, 8)
    qd16 = moved(qd8, -8)
    half = jax.ShapeDtypeStruct((ROWS, FEAT), BF16)
    f32 = lambda *shape: jax.ShapeDtypeStruct(shape, F32)
    unit = 2 * ROWS * FEAT
    scores, dprob, *sums = kernel(
        query_first, (f32(HEADS, ROWS, FIRST), f32(HEADS, ROWS, FIRST)) + (f32(ROWS, FEAT),) * 3, 2, 8, unit * 3 * FIRST
    )(window, offsets, queries, grad_out, keys, values, kv1, kv2, kv4, kv8)
    pre = kernel(key_first, (f32(HEADS, ROWS, 3 * ROWS),) * 2, 0, 5, unit * 2 * 3 * ROWS)(keys, values, qd2, qd4, qd8)
    attended, stats, lse, delta = kernel(
        query_last,
        (half, f32(STAT_ROWS, ROWS), f32(ROWS, FEAT), f32(ROWS, FEAT)),
        1,
        6,
        unit * 2 * BLOCK,
        (pltpu.VMEM((ROWS, 128), F32),),
        n_any=1,
    )(offsets, queries, grad_out, kv16, *sums, pre[1])
    received = [moved(stats, -by) for by in (1, 2, 4, 8, 16)]
    (grad_q,) = kernel(query_gradient, (half,), 1, 13, unit * FIRST)(
        offsets, queries, grad_out, keys, values, kv1, kv2, kv4, kv8, kv16, scores, dprob, lse, delta
    )
    grad_k, grad_v = kernel(key_last, (half, half), 1, 17, unit * 2 * 6 * ROWS)(
        window, keys, values, queries, grad_out, qd1, qd2, qd4, qd8, qd16, *pre, *received[::-1], stats
    )
    return attended, grad_q, grad_k, grad_v


def solution(mesh):
    split = P(("dp", "ctx"), None)
    return jax.shard_map(
        on_device,
        mesh=mesh,
        in_specs=(split, split, split, split, P(), split),
        out_specs=(split,) * 4,
        check_vma=False,
    )
```

```python
import jax
import jax.numpy as jnp
from jax import lax
from jax.experimental import pallas as pl
from jax.experimental.pallas import tpu as pltpu
from jax.sharding import PartitionSpec as P

HEADS = 4
HEAD_DIM = 128
FEAT = HEADS * HEAD_DIM
ROWS = 256
BLOCK = 64
BLOCKS = ROWS // BLOCK
LEVELS = 4
SCALE = HEAD_DIM**-0.5
MASKED = -1e30
STAT_ROWS = 16
WINDOW = ROWS + BLOCK
FIRST = WINDOW + (LEVELS - 1) * BLOCK
HALF = ROWS // 2
WIDE = ROWS + HALF
F32 = jnp.float32
BF16 = jnp.bfloat16


def rows_by_rows(a, b):
    return lax.dot_general(a, b, (((1,), (1,)), ((), ())), preferred_element_type=F32)


def rows_by_columns(a, b):
    return lax.dot_general(a, b, (((1,), (0,)), ((), ())), preferred_element_type=F32)


class Rows:
    def __init__(self, top, bottom):
        self.top, self.bottom = top, bottom

    def __getitem__(self, index):
        rows, columns = index
        if rows.start >= ROWS:
            return self.bottom[rows.start - ROWS : rows.stop - ROWS, columns]
        return self.top[rows, columns]


def picks_of(off, p):
    rows = []
    for j in range(LEVELS):
        picked = jnp.clip(BLOCKS * 2 ** (j + 1) + p - off[p, j], 0, BLOCKS - 1)
        rows.append(pl.multiple_of(picked * BLOCK, BLOCK))
    return rows


def across(column, width):
    return jnp.broadcast_to(column, (column.shape[0], width))


def widened(rows, width):
    return jnp.concatenate([rows] * (-(-width // 128)), 1)[:, :width]


def head_columns(h):
    return slice(HEAD_DIM * h, HEAD_DIM * (h + 1))


def with_ones(v):
    return jnp.concatenate([v, jnp.ones((v.shape[0], HEAD_DIM), BF16)], 1)


def first_keys(p, head, base, own, before, levels, picks):
    parts = [before[base + BLOCK * p : base + ROWS, head], own[base : base + BLOCK * (p + 1), head]]
    for j, ref in enumerate(levels):
        parts.append(ref[pl.ds(base + picks[j], BLOCK), head])
    return jnp.concatenate(parts, 0)


def first_bias(p, rank, length):
    row = lax.broadcasted_iota(jnp.int32, (BLOCK, FIRST), 0)
    col = lax.broadcasted_iota(jnp.int32, (BLOCK, FIRST), 1)
    gap = col - row
    need = jnp.where(col + BLOCK * p < ROWS, 1, 0)
    for j in range(LEVELS - 1):
        need = jnp.where(col >= WINDOW + BLOCK * j, 2 ** (j + 1), need)
    near = (gap <= ROWS) & (gap > ROWS - length)
    return jnp.where((near | (col >= WINDOW)) & (rank >= need), F32(0), F32(MASKED))


def query_first(win, off, q, do, k0, v0, kv1, kv2, kv4, kv8, scores_out, dprob_out, acc, top_out, total_out):
    rank = lax.axis_index("ctx")
    levels = (kv2, kv4, kv8)
    heads = range(HEADS)
    qd, kv0 = Rows(q, do), Rows(k0, v0)
    for p in range(BLOCKS):
        picks = picks_of(off, p)
        mine = slice(BLOCK * p, BLOCK * (p + 1))
        theirs = slice(ROWS + BLOCK * p, ROWS + BLOCK * (p + 1))
        k = [first_keys(p, head_columns(h), 0, kv0, kv1, levels, picks) for h in heads]
        v = [first_keys(p, head_columns(h), ROWS, kv0, kv1, levels, picks) for h in heads]
        scores = [rows_by_rows(qd[mine, head_columns(h)], k[h]) for h in heads]
        scores = [scores[h] * SCALE + first_bias(p, rank, win[h]) for h in heads]
        top = [across(jnp.max(s, 1, keepdims=True), HEAD_DIM) for s in scores]
        for h in heads:
            scores_out[h, mine, :] = scores[h]
            dprob_out[h, mine, :] = rows_by_rows(qd[theirs, head_columns(h)], v[h])
        weights = [jnp.exp(scores[h] - widened(top[h], FIRST)).astype(BF16) for h in heads]
        sums = [rows_by_columns(weights[h], with_ones(v[h])) for h in heads]
        for h in heads:
            acc[mine, head_columns(h)] = sums[h][:, :HEAD_DIM]
            total_out[mine, head_columns(h)] = sums[h][:, HEAD_DIM:]
            top_out[mine, head_columns(h)] = top[h]


def query_last(off, q, do, kv16, acc, top0, total0, _, att, stats, lse_out, delta_out, tall):
    rank = lax.axis_index("ctx")
    heads = range(HEADS)
    qd = Rows(q, do)
    lane = lax.broadcasted_iota(jnp.int32, (BLOCK, 128), 1)
    bias = jnp.where(rank >= 2**LEVELS, F32(0), F32(MASKED))
    tiles = [(p, h) for p in range(BLOCKS) for h in heads]
    picks = [picks_of(off, p)[LEVELS - 1] for p in range(BLOCKS)]
    rows = lambda p, base=0: slice(base + BLOCK * p, base + BLOCK * (p + 1))
    at = lambda ref, p, h: ref[rows(p), head_columns(h)]
    scores = [
        rows_by_rows(at(qd, p, h), kv16[pl.ds(picks[p], BLOCK), head_columns(h)]) * SCALE + bias for p, h in tiles
    ]
    before = [at(top0, p, h) for p, h in tiles]
    top = [jnp.maximum(b, across(jnp.max(s, 1, keepdims=True), HEAD_DIM)) for b, s in zip(before, scores)]
    weights = [jnp.exp(s - t[:, :BLOCK]).astype(BF16) for s, t in zip(scores, top)]
    sums = [
        rows_by_columns(w, with_ones(kv16[pl.ds(ROWS + picks[p], BLOCK), head_columns(h)]))
        for w, (p, h) in zip(weights, tiles)
    ]
    fade = [jnp.exp(b - t) for b, t in zip(before, top)]
    total = [at(total0, p, h) * f + x[:, HEAD_DIM:] for f, x, (p, h) in zip(fade, sums, tiles)]
    out = [at(acc, p, h) * f + x[:, :HEAD_DIM] for f, x, (p, h) in zip(fade, sums, tiles)]
    out = [(o * (1.0 / t)).astype(BF16) for o, t in zip(out, total)]
    lse = [t + jnp.log(x) for t, x in zip(top, total)]
    delta = [
        across(jnp.sum(qd[rows(p, ROWS), head_columns(h)].astype(F32) * o.astype(F32), 1, keepdims=True), HEAD_DIM)
        for o, (p, h) in zip(out, tiles)
    ]
    for p in range(BLOCKS):
        kept = jnp.zeros((BLOCK, 128), F32)
        for h in heads:
            i = p * HEADS + h
            att[rows(p), head_columns(h)] = out[i]
            lse_out[rows(p), head_columns(h)] = lse[i]
            delta_out[rows(p), head_columns(h)] = delta[i]
            kept = jnp.where(lane == h, lse[i], kept)
            kept = jnp.where(lane == HEADS + h, delta[i], kept)
        tall[rows(p), :] = kept
    stats[0 : 2 * HEADS, :] = tall[...].T[0 : 2 * HEADS]
    wide_row = lax.broadcasted_iota(jnp.int32, (STAT_ROWS - 2 * HEADS, ROWS), 0)
    wide_block = lax.broadcasted_iota(jnp.int32, (STAT_ROWS - 2 * HEADS, ROWS), 1) // BLOCK
    chosen = jnp.zeros((STAT_ROWS - 2 * HEADS, ROWS), F32)
    for p in range(BLOCKS):
        for j in range(LEVELS):
            picked = jnp.clip(BLOCKS * 2 ** (j + 1) + p - off[p, j], 0, BLOCKS - 1)
            chosen = jnp.where((wide_row == j) & (wide_block == p), picked.astype(F32), chosen)
    stats[2 * HEADS :, :] = chosen


def query_gradient(off, q, do, k0, v0, kv1, kv2, kv4, kv8, kv16, scores, dprob, lse, delta, dq):
    rank = lax.axis_index("ctx")
    levels = (kv2, kv4, kv8)
    qd, kv0 = Rows(q, do), Rows(k0, v0)
    heads = range(HEADS)
    bias = jnp.where(rank >= 2**LEVELS, F32(0), F32(MASKED))
    for p in range(BLOCKS):
        picks = picks_of(off, p)
        mine = slice(BLOCK * p, BLOCK * (p + 1))
        theirs = slice(ROWS + BLOCK * p, ROWS + BLOCK * (p + 1))
        k = [first_keys(p, head_columns(h), 0, kv0, kv1, levels, picks) for h in heads]
        last_k = [kv16[pl.ds(picks[-1], BLOCK), head_columns(h)] for h in heads]
        last_v = [kv16[pl.ds(ROWS + picks[-1], BLOCK), head_columns(h)] for h in heads]
        last = [rows_by_rows(qd[mine, head_columns(h)], last_k[h]) * SCALE + bias for h in heads]
        last_dprob = [rows_by_rows(qd[theirs, head_columns(h)], last_v[h]) for h in heads]
        my_lse = [lse[mine, head_columns(h)] for h in heads]
        my_delta = [delta[mine, head_columns(h)] for h in heads]
        first = [
            jnp.exp(scores[h, mine, :] - widened(my_lse[h], FIRST)) * (dprob[h, mine, :] - widened(my_delta[h], FIRST))
            for h in heads
        ]
        last = [jnp.exp(last[h] - my_lse[h][:, :BLOCK]) * (last_dprob[h] - my_delta[h][:, :BLOCK]) for h in heads]
        for h in heads:
            total = rows_by_columns(first[h].astype(BF16), k[h]) + rows_by_columns(last[h].astype(BF16), last_k[h])
            dq[mine, head_columns(h)] = (total * SCALE).astype(BF16)


def joined(a, b, base, cut, head):
    return jnp.concatenate([a[base + cut : base + ROWS, head], b[base : base + cut + HALF, head]], 0)


def key_first(k0, v0, qd2, qd4, qd8, scores, dprob):
    kv = Rows(k0, v0)
    for h in range(HEADS):
        head = head_columns(h)
        for j, qd in enumerate((qd2, qd4, qd8)):
            columns = slice(ROWS * j, ROWS * (j + 1))
            scores[h, :, columns] = rows_by_rows(kv[0:ROWS, head], qd[0:ROWS, head]) * SCALE
            dprob[h, :, columns] = rows_by_rows(kv[ROWS : 2 * ROWS, head], qd[ROWS : 2 * ROWS, head])


def key_last(
    win, k0, v0, q0, do0, qd1, qd2, qd4, qd8, qd16, far_scores, far_dprob, st16, st8, st4, st2, st1, st0, dk, dv
):
    kv, qd0 = Rows(k0, v0), Rows(q0, do0)
    key_block = (lax.broadcasted_iota(jnp.int32, (ROWS, ROWS), 0) // BLOCK).astype(F32)
    far = ((qd2, st2), (qd4, st4), (qd8, st8), (qd16, st16))
    row = lax.broadcasted_iota(jnp.int32, (HALF, WIDE), 0)
    col = lax.broadcasted_iota(jnp.int32, (HALF, WIDE), 1)
    gap = col - row
    chosen = [key_block == st[2 * HEADS + j : 2 * HEADS + j + 1, :] for j, (_, st) in enumerate(far)]
    for h in range(HEADS):
        head = head_columns(h)
        lanes = lambda r, cut: jnp.concatenate([st0[r : r + 1, cut:ROWS], st1[r : r + 1, 0 : cut + HALF]], 1)
        bias = jnp.where((gap >= 0) & (gap < win[h]), F32(0), F32(MASKED))
        scores = [
            rows_by_rows(kv[HALF * c : HALF * (c + 1), head], joined(qd0, qd1, 0, HALF * c, head)) * SCALE + bias
            for c in range(2)
        ]
        dprob = [
            rows_by_rows(kv[ROWS + HALF * c : ROWS + HALF * (c + 1), head], joined(qd0, qd1, ROWS, HALF * c, head))
            for c in range(2)
        ]
        scores += [far_scores[h, :, ROWS * j : ROWS * (j + 1)] for j in range(LEVELS - 1)]
        dprob += [far_dprob[h, :, ROWS * j : ROWS * (j + 1)] for j in range(LEVELS - 1)]
        scores.append(rows_by_rows(kv[0:ROWS, head], qd16[0:ROWS, head]) * SCALE)
        dprob.append(rows_by_rows(kv[ROWS : 2 * ROWS, head], qd16[ROWS : 2 * ROWS, head]))
        lse = [lanes(h, HALF * c) for c in range(2)] + [st[h : h + 1, :] for _, st in far]
        delta = [lanes(HEADS + h, HALF * c) for c in range(2)]
        delta += [st[HEADS + h : HEADS + h + 1, :] for _, st in far]
        probs = [jnp.exp(scores[i] - lse[i]) for i in range(2)]
        probs += [jnp.exp(jnp.where(chosen[j], scores[2 + j] - lse[2 + j], F32(MASKED))) for j in range(LEVELS)]
        dscore = [(probs[i] * (dprob[i] - delta[i])).astype(BF16) for i in range(2 + LEVELS)]
        probs = [x.astype(BF16) for x in probs]
        for rows, base, out, scale in ((dscore, 0, dk, SCALE), (probs, ROWS, dv, 1.0)):
            near = [rows_by_columns(rows[c], joined(qd0, qd1, base, HALF * c, head)) for c in range(2)]
            stack = jnp.concatenate([qd[base : base + ROWS, head] for qd, _ in far], 0)
            total = jnp.concatenate(near, 0) + rows_by_columns(jnp.concatenate(rows[2:], 1), stack)
            out[:, head] = (total * scale).astype(BF16)


def moved(array, by):
    size = lax.axis_size("ctx")
    return lax.ppermute(array, "ctx", [(i, i + by) for i in range(size) if 0 <= i + by < size])


def swapped(array, bit):
    size = lax.axis_size("ctx")
    return lax.ppermute(array, "ctx", [(i, i ^ bit) for i in range(size)])


def passed(array):
    anywhere = pl.BlockSpec(memory_space=pl.ANY)
    return pl.pallas_call(
        lambda a, b: None,
        out_shape=jax.ShapeDtypeStruct(array.shape, array.dtype),
        in_specs=[anywhere],
        out_specs=anywhere,
        input_output_aliases={0: 0},
        compiler_params=pltpu.CompilerParams(vmem_limit_bytes=2**20),
        cost_estimate=pl.CostEstimate(flops=10**10, bytes_accessed=4 * 10**7, transcendentals=0),
        name="passed",
    )(array)


def pack(*refs):
    count = len(refs) * 2 // 3
    for i in range(count):
        refs[count + i // 2][ROWS * (i % 2) : ROWS * (i % 2 + 1), :] = refs[i][...]


def packed(*arrays):
    vmem = pl.BlockSpec(memory_space=pltpu.VMEM)
    pair = jax.ShapeDtypeStruct((2 * ROWS, FEAT), BF16)
    return pl.pallas_call(
        pack,
        out_shape=(pair,) * (len(arrays) // 2),
        in_specs=[vmem] * len(arrays),
        out_specs=(vmem,) * (len(arrays) // 2),
        compiler_params=pltpu.CompilerParams(vmem_limit_bytes=8 * 2**20),
        cost_estimate=pl.CostEstimate(flops=0, bytes_accessed=len(arrays) * ROWS * FEAT * 4, transcendentals=0),
        name="pack",
    )(*arrays)


def kernel(body, out_shape, n_smem, n_vmem, flops, scratch=(), n_any=0):
    smem = pl.BlockSpec(memory_space=pltpu.SMEM)
    vmem = pl.BlockSpec(memory_space=pltpu.VMEM)
    return pl.pallas_call(
        body,
        out_shape=tuple(out_shape),
        in_specs=[smem] * n_smem + [vmem] * n_vmem + [pl.BlockSpec(memory_space=pl.ANY)] * n_any,
        out_specs=(vmem,) * len(out_shape),
        scratch_shapes=list(scratch),
        compiler_params=pltpu.CompilerParams(vmem_limit_bytes=32 * 2**20),
        cost_estimate=pl.CostEstimate(flops=flops, bytes_accessed=n_vmem * ROWS * FEAT * 4, transcendentals=0),
        name=body.__name__,
    )


def on_device(queries, keys, values, grad_out, window, offsets):
    rank = lax.axis_index("ctx")
    (kv0,) = packed(keys, values)
    (qd0,) = packed(queries, grad_out)
    kv4 = moved(kv0, 4)
    qd4 = moved(qd0, -4)
    kv2 = swapped(jnp.where(rank % 4 < 2, kv0, kv4), 2)
    qd2 = swapped(jnp.where(rank % 4 < 2, qd4, qd0), 2)
    kv1 = swapped(jnp.where(rank % 2 == 0, kv0, kv2), 1)
    qd1 = swapped(jnp.where(rank % 2 == 0, qd2, qd0), 1)
    kv8 = passed(moved(kv4, 4))
    qd8 = passed(moved(qd4, -4))
    kv16 = moved(kv8, 8)
    qd16 = moved(qd8, -8)
    half = jax.ShapeDtypeStruct((ROWS, FEAT), BF16)
    f32 = lambda *shape: jax.ShapeDtypeStruct(shape, F32)
    unit = 2 * ROWS * FEAT
    scores, dprob, *sums = kernel(
        query_first, (f32(HEADS, ROWS, FIRST), f32(HEADS, ROWS, FIRST)) + (f32(ROWS, FEAT),) * 3, 2, 8, unit * 3 * FIRST
    )(window, offsets, queries, grad_out, keys, values, kv1, kv2, kv4, kv8)
    pre = kernel(key_first, (f32(HEADS, ROWS, 3 * ROWS),) * 2, 0, 5, unit * 2 * 3 * ROWS)(keys, values, qd2, qd4, qd8)
    attended, stats, lse, delta = kernel(
        query_last,
        (half, f32(STAT_ROWS, ROWS), f32(ROWS, FEAT), f32(ROWS, FEAT)),
        1,
        6,
        unit * 2 * BLOCK,
        (pltpu.VMEM((ROWS, 128), F32),),
        n_any=1,
    )(offsets, queries, grad_out, kv16, *sums, pre[1])
    received = [moved(stats, -by) for by in (1, 2, 4, 8, 16)]
    (grad_q,) = kernel(query_gradient, (half,), 1, 13, unit * FIRST)(
        offsets, queries, grad_out, keys, values, kv1, kv2, kv4, kv8, kv16, scores, dprob, lse, delta
    )
    grad_k, grad_v = kernel(key_last, (half, half), 1, 17, unit * 2 * 6 * ROWS)(
        window, keys, values, queries, grad_out, qd1, qd2, qd4, qd8, qd16, *pre, *received[::-1], stats
    )
    return attended, grad_q, grad_k, grad_v


def solution(mesh):
    split = P(("dp", "ctx"), None)
    return jax.shard_map(
        on_device,
        mesh=mesh,
        in_specs=(split, split, split, split, P(), split),
        out_specs=(split,) * 4,
        check_vma=False,
    )
```
